32 devices in a mesh: gx: 8 (over z, core), gy: 4 (over y, x).
Axes of the slice: x: 2, y: 2, z: 4, core: 2. Of those that a mesh axis runs over, the one named last changes fastest.
Arguments:
- member_flows: float32 [24, 4, 64, 32, 128], P(None, None, 'gx', 'gy'), may hold values from -6 to 6
- wall_texture: float32 [24, 64, 32], P(None, 'gx', 'gy'), may hold values from 0.2 to 2
- cross_link_matrix: float32 [4, 4], replicated, may hold values from -3 to 3
- obs_owner: int32 [4, 4096], replicated, may hold values from 0 to 31
- obs_cell: int32 [4, 4096], replicated, may hold values from 0 to 8191
- obs_value: float32 [4, 4096], replicated, may hold values from -8 to 8
- obs_var: float32 [4, 4096], replicated, may hold values from 0.1 to 1
- local_mask: int32 [4, 8, 4, 64], P(None, 'gx', 'gy'), may hold values 0 or 1
Outputs:
- analysis: float32 [24, 4, 64, 32, 128], P(None, None, 'gx', 'gy')
- rough_post: float32 [24, 64, 32], P(None, 'gx', 'gy')
The draws below stay inside these ranges and needn't reach their ends.
Inputs may be any that keep to these rules, and one draw needn't show every extreme that they name: `obs_owner`: observations are skewed towards a few tiles.
All inputs are finite; a program needn't handle non-finite values. No bound on the sum of `local_mask` on one device may be relied on, other than what follows from the above.
Results may differ from the reference program's by a relative error of at most 0.0003.
Values sent between devices are 32-bit elements; how exact they have to be, the bound alone decides.
A program may use at most 64 MiB of HBM per device.

```python
import math
import jax
import jax.numpy as jnp
import numpy as np
from jax import lax

MEMBERS = 24
FIELDS = 4
CX = 8
CY = 8
NZ = 128
BATCHES = 4
OBS = 4096
OBS_BLOCK = 64
NB = 64
STREAMWISE_TILES = 8
SPANWISE_TILES = 4
TILES = 32
NX = 64
NY = 32
N_GX = 8
N_GY = 4


def plant(drawn, rng, least, high):
    longest = drawn.shape.index(max(drawn.shape))
    spots = []
    for shift in (0, 1):
        where = [jax.random.randint(jax.random.fold_in(rng, axis), (), 0, length) for axis, length in enumerate(drawn.shape)]
        where[longest] = (where[longest] + shift) % drawn.shape[longest]
        spots.append(tuple(where))
    return drawn.at[spots[0]].set(least).at[spots[1]].set(high)


def steps_of(own_key, shape, pieces, low, high):
    def one(axis_at, shards_of):
        steps = jax.random.uniform(jax.random.fold_in(jax.random.fold_in(own_key, 6), axis_at), (shards_of,), jnp.float32, low / len(pieces), high / len(pieces))
        return jnp.repeat(jnp.exp(steps), shape[axis_at] // shards_of).reshape((-1,) + (1,) * (len(shape) - axis_at - 1))

    gain = one(*pieces[0])
    for cut in pieces[1:]:
        gain = gain * one(*cut)
    return gain


def cumulative_ranks(count, lean):
    weights = [(1 << 20) // math.isqrt(standing ** lean) + 1 for standing in range(1, count + 1)]
    scale = 1 + sum(weights) // (1 << 30)
    return np.cumsum(np.array([max(1, weight // scale) for weight in weights]))


def ranked(own_key, dims, count, lean):
    listing = cumulative_ranks(count, lean)
    lot = jax.random.randint(jax.random.fold_in(own_key, 1), dims, 0, int(listing[count - 1]))
    standing = jnp.searchsorted(jnp.asarray(listing, jnp.int32), lot, side="right")
    return jax.random.permutation(jax.random.fold_in(own_key, 2), count)[standing].astype(jnp.int32)


def bell_draw(key, extent, scale, reach, shards=(), held_as=jnp.bfloat16):
    drawn = jax.random.normal(key, extent, jnp.float32) * scale
    if len(shards) > 0:
        drawn = steps_of(key, extent, shards, -0.22, 0.18) * drawn
    return jnp.clip(drawn, min=-reach, max=reach).astype(held_as)


def setup_inputs(seed: int = 0) -> dict:
    splits = jax.random.split(jax.random.key(seed), 9)
    return {
        "member_flows": bell_draw(splits[0], (MEMBERS, FIELDS, NX, NY, NZ), 1.0, 6.0, ((2, 8), (3, 4)), jnp.float32),
        "wall_texture": jnp.clip(jnp.exp(math.log(2.0) - 2.3025851 * jax.random.uniform(splits[1], (MEMBERS, NX, NY), jnp.float32) ** steps_of(splits[1], (MEMBERS, NX, NY), ((1, 8), (2, 4)), -0.2, 0.2)), 0.2, 2.0),
        "cross_link_matrix": bell_draw(splits[2], (FIELDS, FIELDS), FIELDS ** -0.5, 3.0, (), jnp.float32),
        "obs_owner": plant(ranked(splits[3], (BATCHES, OBS), TILES, 2), jax.random.fold_in(splits[3], 3), 0, TILES - 1).astype(jnp.int32),
        "obs_cell": plant(jax.random.randint(splits[4], (BATCHES, OBS), 0, CX * CY * NZ), jax.random.fold_in(splits[4], 1), 0, (CX * CY * NZ) - 1).astype(jnp.int32),
        "obs_value": bell_draw(splits[5], (BATCHES, OBS), 1.5, 8.0, (), jnp.float32),
        "obs_var": jnp.clip(jnp.exp(jax.random.uniform(splits[6], (BATCHES, OBS), jnp.float32, math.log(0.1), math.log(1.0))), 0.1, 1.0),
        "local_mask": plant((jax.random.randint(splits[7], (BATCHES, STREAMWISE_TILES, SPANWISE_TILES, NB), 0, 2) < 1).astype(jnp.int32), jax.random.fold_in(splits[7], 1), 0, 1),
    }


def prior_flow_vector(flow_grids, wall_texture_entries, cross_link_matrix):
    padded = jnp.pad(flow_grids, ((0, 0), (1, 1), (1, 1), (1, 1)))
    center = padded[:, 1:-1, 1:-1, 1:-1]
    lap = padded[:, 2:, 1:-1, 1:-1] + padded[:, :-2, 1:-1, 1:-1]
    lap = lap + padded[:, 1:-1, 2:, 1:-1] + padded[:, 1:-1, :-2, 1:-1]
    lap = lap + padded[:, 1:-1, 1:-1, 2:] + padded[:, 1:-1, 1:-1, :-2] - 6.0 * center
    slope = 0.5 * (padded[:, 2:, 1:-1, 1:-1] - padded[:, :-2, 1:-1, 1:-1])
    mixed = jnp.einsum('fg,gxyz->fxyz', cross_link_matrix, center, precision=lax.Precision.HIGHEST)
    level = (jnp.arange(center.shape[-1]) == 0).astype(center.dtype)
    drag = wall_texture_entries[None, :, :, None] * center * level
    return center + 0.5 * (0.15 * lap - 0.6 * slope + mixed - drag)

def reference(member_flows, wall_texture, cross_link_matrix, obs_owner, obs_cell, obs_value, obs_var, local_mask):
    members = member_flows.shape[0]
    member_flow_vector = lax.map(lambda subdomain_couple: prior_flow_vector(subdomain_couple[0], subdomain_couple[1], cross_link_matrix), (member_flows, wall_texture))
    tiles = member_flow_vector.reshape(members, FIELDS, N_GX, CX, N_GY, CY, NZ).transpose(2, 4, 0, 1, 3, 5, 6)
    rtiles = wall_texture.reshape(members, N_GX, CX, N_GY, CY).transpose(1, 3, 0, 2, 4)
    for batch in range(BATCHES):
        owner = obs_owner[batch]
        cell = obs_cell[batch]
        tile_x = owner // N_GY
        tile_y = owner % N_GY
        loc_x = cell // (CY * NZ)
        loc_y = cell // NZ % CY
        loc_z = cell % NZ
        values = tiles[tile_x, tile_y, :, 0, loc_x, loc_y, loc_z]
        ybar = lax.optimization_barrier(jnp.mean(values, axis=1))
        dev = values - ybar[:, None]
        spread = lax.optimization_barrier(jnp.sum(dev * dev, axis=1)) / (members - 1.0)
        ovar = obs_var[batch]
        root = jnp.sqrt(spread + ovar)
        innov = obs_value[batch] - ybar
        gterm = (innov / (spread + ovar))[:, None] - dev / (root * (jnp.sqrt(ovar) + root))[:, None]
        blocks = jnp.einsum('jbn,jbm->jnm', dev.reshape(NB, OBS_BLOCK, members), gterm.reshape(NB, OBS_BLOCK, members), precision=lax.Precision.HIGHEST) / (members - 1.0)
        weights = jnp.einsum('tuj,jnm->tunm', local_mask[batch].astype(jnp.float32), blocks, precision=lax.Precision.HIGHEST)
        prime = tiles - lax.optimization_barrier(jnp.mean(tiles, axis=2, keepdims=True))
        tiles = tiles + jnp.einsum('tunm,tunfxyz->tumfxyz', weights, prime, precision=lax.Precision.HIGHEST)
        rprime = rtiles - lax.optimization_barrier(jnp.mean(rtiles, axis=2, keepdims=True))
        rtiles = rtiles + jnp.einsum('tunm,tunxy->tumxy', weights, rprime, precision=lax.Precision.HIGHEST)
    analysis = tiles.transpose(2, 3, 0, 4, 1, 5, 6).reshape(members, FIELDS, N_GX * CX, N_GY * CY, NZ)
    rough_post = rtiles.transpose(2, 0, 3, 1, 4).reshape(members, N_GX * CX, N_GY * CY)
    return (analysis, rough_post)
```

```python
import functools

import jax
import jax.numpy as jnp
from jax import lax
from jax.experimental import pallas as pl
from jax.experimental.pallas import tpu as pltpu
from jax.sharding import PartitionSpec as P

OBS_BLOCK = 64
F32 = jnp.float32
BF16 = jnp.bfloat16
NT = (((1,), (1,)), ((), ()))


def pieces(x):
    high = x.astype(BF16).astype(F32)
    return high, x - high


def stacked_dot(left, right):
    lh, ll = pieces(left)
    rh, rl = pieces(right)
    lhs = jnp.concatenate([lh, lh, ll], axis=1).astype(BF16)
    rhs = jnp.concatenate([rh, rl, rh], axis=0).astype(BF16)
    return jnp.dot(lhs, rhs, preferred_element_type=F32)


def halo(block, axis, dim):
    count = lax.axis_size(axis)
    forward = [(i, i + 1) for i in range(count - 1)]
    backward = [(target, source) for source, target in forward]
    size = block.shape[dim]
    low = lax.ppermute(lax.slice_in_dim(block, size - 1, size, axis=dim), axis, forward)
    high = lax.ppermute(lax.slice_in_dim(block, 0, 1, axis=dim), axis, backward)
    return low, high


def forecast_kernel(matrix_ref, c_ref, xlo_ref, xhi_ref, ylo_ref, yhi_ref, wall_ref, out_ref):
    members, fields, cx, cy, nz = c_ref.shape
    sub = lax.broadcasted_iota(jnp.int32, (cy, nz), 0)
    lane = lax.broadcasted_iota(jnp.int32, (cy, nz), 1)

    def one(m, carry):
        for x in range(cx):
            cells = [c_ref[m, f, x] for f in range(fields)]
            wall = jnp.where(lane == 0, jnp.broadcast_to(wall_ref[m][:, x : x + 1], (cy, nz)), 0.0)
            for f in range(fields):
                c = cells[f]
                before = c_ref[m, f, x - 1] if x > 0 else xlo_ref[m, f]
                after = c_ref[m, f, x + 1] if x < cx - 1 else xhi_ref[m, f]
                lap = before + after
                lap = lap + jnp.where(sub == cy - 1, yhi_ref[m, f, x : x + 1], pltpu.roll(c, cy - 1, 0))
                lap = lap + jnp.where(sub == 0, ylo_ref[m, f, x : x + 1], pltpu.roll(c, 1, 0))
                lap = lap + jnp.where(lane == nz - 1, 0.0, pltpu.roll(c, nz - 1, 1))
                lap = lap + jnp.where(lane == 0, 0.0, pltpu.roll(c, 1, 1)) - 6.0 * c
                slope = 0.5 * (after - before)
                mixed = matrix_ref[f, 0] * cells[0]
                for g in range(1, fields):
                    mixed = mixed + matrix_ref[f, g] * cells[g]
                out_ref[m, f, x] = c + 0.5 * (0.15 * lap - 0.6 * slope + mixed - wall * c)
        return carry

    lax.fori_loop(0, members, one, 0)


def forecast(c, wall_texture, matrix):
    members, fields, cx, cy, nz = c.shape
    xlo, xhi = halo(c, "gx", 2)
    ylo, yhi = halo(c, "gy", 3)
    vmem = pl.BlockSpec(memory_space=pltpu.VMEM)
    return pl.pallas_call(
        forecast_kernel,
        out_shape=jax.ShapeDtypeStruct(c.shape, F32),
        in_specs=[pl.BlockSpec(memory_space=pltpu.SMEM)] + [vmem] * 6,
        out_specs=vmem,
        compiler_params=pltpu.CompilerParams(vmem_limit_bytes=40 * 2**20),
        name="forecast",
    )(
        matrix,
        c,
        xlo.reshape(members, fields, cy, nz),
        xhi.reshape(members, fields, cy, nz),
        ylo.reshape(members, fields, cx, nz),
        yhi.reshape(members, fields, cx, nz),
        wall_texture.transpose(0, 2, 1),
    )


def pick_kernel(nz, field_ref, cell_ref, out_ref, wide_ref):
    members, count = out_ref.shape
    rows = field_ref.shape[0] // members
    cell = cell_ref[0]
    z = lax.rem(cell, nz)
    row = lax.div(cell, nz)
    level = lax.rem(lax.broadcasted_iota(jnp.int32, (2 * nz, count), 0), nz)
    hot = jnp.where(level == z, 1.0, 0.0).astype(BF16)
    wide_ref[...] = jnp.dot(field_ref[...], hot, preferred_element_type=F32)
    total = jnp.zeros((members, count), F32)
    for r in range(rows):
        total = jnp.where(row == r, wide_ref[r * members : (r + 1) * members], total)
    out_ref[...] = total


def pick(first, cells):
    members, rows, nz = first.shape
    batches, obs = cells.shape
    turned = first.transpose(1, 0, 2).reshape(rows * members, nz)
    high = lax.reduce_precision(turned, 8, 7)
    low = (turned - high).astype(BF16)
    high = high.astype(BF16)
    count = min(256, obs)
    return pl.pallas_call(
        functools.partial(pick_kernel, nz),
        grid=(batches, obs // count),
        out_shape=jax.ShapeDtypeStruct((batches, members, obs), F32),
        in_specs=[
            pl.BlockSpec((rows * members, 2 * nz), lambda b, i: (0, 0)),
            pl.BlockSpec((None, 1, count), lambda b, i: (b, 0, i)),
        ],
        out_specs=pl.BlockSpec((None, members, count), lambda b, i: (b, 0, i)),
        scratch_shapes=[pltpu.VMEM((rows * members, count), F32)],
        compiler_params=pltpu.CompilerParams(vmem_limit_bytes=32 * 2**20),
        name="pick",
    )(jnp.concatenate([high, low], axis=1), cells[:, None, :])


def window_kernel(
    axes, y_ref, own_ref, value_ref, var_ref, mask_ref, out_ref, part_ref, send_ref, land_ref, send_sem, land_sem
):
    nx, ny = axes
    n = nx * ny
    batches, members, obs = y_ref.shape
    blocks = obs // OBS_BLOCK
    groups = members // 8
    per = min(4, blocks)
    width = per * OBS_BLOCK
    me = lax.axis_index("gx") * ny + lax.axis_index("gy")

    def coords(t):
        return {"gx": lax.div(t, ny), "gy": lax.rem(t, ny)}

    barrier = pltpu.get_barrier_semaphore()

    def greet(d, carry):
        pl.semaphore_signal(
            barrier, inc=1, device_id=coords(lax.rem(me + d, n)), device_id_type=pl.DeviceIdType.MESH
        )
        return carry

    lax.fori_loop(1, n, greet, 0)
    pl.semaphore_wait(barrier, n - 1)

    block_of = lax.broadcasted_iota(jnp.int32, (8, width), 1) // OBS_BLOCK
    group_of = lax.broadcasted_iota(jnp.int32, (8, 128), 1) // members
    eye = jnp.where(
        lax.broadcasted_iota(jnp.int32, (members, members), 0)
        == lax.broadcasted_iota(jnp.int32, (members, members), 1),
        1.0,
        0.0,
    )

    def one(b, mix):
        for c in range(obs // width):
            at = pl.ds(c * width, width)
            y = stacked_dot(mix, y_ref[b, :, at])
            ybar = jnp.sum(y, axis=0, keepdims=True) / members
            dev = y - ybar
            spread = jnp.sum(dev * dev, axis=0, keepdims=True) / (members - 1.0)
            var = var_ref[b, :, at]
            total = spread + var
            root = jnp.sqrt(total)
            g = (value_ref[b, :, at] - ybar) / total - dev * (1.0 / (root * (jnp.sqrt(var) + root)))
            g = jnp.where(own_ref[b, :, at] > 0, g, 0.0)
            lhs = jnp.concatenate(
                [
                    jnp.where(block_of == j, g[8 * i : 8 * i + 8], 0.0)
                    for i in range(groups)
                    for j in range(per)
                ],
                axis=0,
            )
            rhs = jnp.concatenate([dev] * groups + [jnp.zeros((128 - groups * members, width), F32)], axis=0)
            lh, ll = pieces(lhs)
            rh, rl = pieces(rhs)
            lh, ll, rh, rl = (a.astype(BF16) for a in (lh, ll, rh, rl))
            dot = functools.partial(lax.dot_general, dimension_numbers=NT, preferred_element_type=F32)
            both = dot(lh, rh) + (dot(lh, rl) + dot(ll, rh))
            for j in range(per):
                tile = jnp.zeros((8, 128), F32)
                for i in range(groups):
                    k = (i * per + j) * 8
                    tile = jnp.where(group_of == i, both[k : k + 8], tile)
                part_ref[c * per + j] = tile
        mask = mask_ref[b].astype(F32)
        mask2 = jnp.concatenate([mask, mask], axis=1).astype(BF16)
        for q in range(8):
            high, low = pieces(part_ref[:, q, :])
            send_ref[b, :, q, :] = jnp.dot(
                mask2, jnp.concatenate([high, low], axis=0).astype(BF16), preferred_element_type=F32
            )

        def push(d, carry):
            to = lax.rem(me + d, n)
            pltpu.make_async_remote_copy(
                src_ref=send_ref.at[b, to],
                dst_ref=land_ref.at[b, d - 1],
                send_sem=send_sem.at[b],
                recv_sem=land_sem.at[b],
                device_id=coords(to),
                device_id_type=pl.DeviceIdType.MESH,
            ).start()
            return carry

        lax.fori_loop(1, n, push, 0)
        pltpu.make_async_copy(land_ref.at[b], land_ref.at[b], land_sem.at[b]).wait()
        zsum = send_ref[b, me] + jnp.sum(land_ref[b], axis=0)
        zt = jnp.concatenate(
            [(zsum if i == 0 else pltpu.roll(zsum, 128 - i * members, 1))[:, :members] for i in range(groups)],
            axis=0,
        ) / (members - 1.0)
        zt = zt - jnp.mean(zt, axis=1, keepdims=True)
        pltpu.make_async_copy(land_ref.at[b], land_ref.at[b], send_sem.at[b]).wait()
        return mix + stacked_dot(zt, mix)

    out_ref[...] = lax.fori_loop(0, batches, one, eye)


def window(axes, y, own, value, var, masks):
    n = axes[0] * axes[1]
    batches, members, obs = y.shape
    vmem = pl.BlockSpec(memory_space=pltpu.VMEM)
    return pl.pallas_call(
        functools.partial(window_kernel, axes),
        out_shape=jax.ShapeDtypeStruct((members, members), F32),
        in_specs=[vmem] * 5,
        out_specs=vmem,
        scratch_shapes=[
            pltpu.VMEM((obs // OBS_BLOCK, 8, 128), F32),
            pltpu.VMEM((batches, n, 8, 128), F32),
            pltpu.VMEM((batches, n - 1, 8, 128), F32),
            pltpu.SemaphoreType.DMA((batches,)),
            pltpu.SemaphoreType.DMA((batches,)),
        ],
        compiler_params=pltpu.CompilerParams(
            collective_id=0, has_side_effects=True, vmem_limit_bytes=40 * 2**20
        ),
        name="window",
    )(y, own[:, None], value[:, None], var[:, None], masks)


def apply_kernel(mix_ref, state_ref, rough_ref, out_ref, rough_out_ref):
    members, fields, cx, cy, nz = state_ref.shape
    mix = mix_ref[...]
    rough_out_ref[...] = stacked_dot(mix, rough_ref[...])
    for x in range(cx):
        for y in range(cy):
            out_ref[:, 0, x, y, :] = stacked_dot(mix, state_ref[:, 0, x, y, :])


def apply(mix, state, rough):
    members, fields, cx, cy, nz = state.shape
    block = pl.BlockSpec((members, 1, cx, cy, nz), lambda f: (0, f, 0, 0, 0))
    flat = rough.reshape(members, cx * cy)
    state, flat = pl.pallas_call(
        apply_kernel,
        grid=(fields,),
        out_shape=(
            jax.ShapeDtypeStruct(state.shape, F32),
            jax.ShapeDtypeStruct(flat.shape, F32),
        ),
        in_specs=[
            pl.BlockSpec((members, members), lambda f: (0, 0)),
            block,
            pl.BlockSpec((members, cx * cy), lambda f: (0, 0)),
        ],
        out_specs=(block, pl.BlockSpec((members, cx * cy), lambda f: (0, 0))),
        compiler_params=pltpu.CompilerParams(vmem_limit_bytes=32 * 2**20),
        name="apply",
    )(mix, state, flat)
    return state, flat.reshape(rough.shape)


def on_device(
    axes,
    member_flows,
    wall_texture,
    cross_link_matrix,
    obs_owner,
    obs_cell,
    obs_value,
    obs_var,
    local_mask,
):
    members, fields, cx, cy, nz = member_flows.shape
    mytile = lax.axis_index("gx") * axes[1] + lax.axis_index("gy")
    masks = lax.all_gather(local_mask[:, 0, 0], ("gx", "gy"), axis=1)
    own = (obs_owner == mytile).astype(jnp.int32)
    state = forecast(member_flows, wall_texture, cross_link_matrix)
    y = pick(state[:, 0].reshape(members, cx * cy, nz), obs_cell)
    mix = window(axes, y, own, obs_value, obs_var, masks)
    return apply(mix, state, wall_texture)


def solution(mesh):
    axes = (mesh.shape["gx"], mesh.shape["gy"])
    return jax.shard_map(
        functools.partial(on_device, axes),
        mesh=mesh,
        in_specs=(
            P(None, None, "gx", "gy", None),
            P(None, "gx", "gy"),
            P(),
            P(),
            P(),
            P(),
            P(),
            P(None, "gx", "gy", None),
        ),
        out_specs=(P(None, None, "gx", "gy", None), P(None, "gx", "gy")),
        check_vma=False,
    )
```

```python
import functools

import jax
import jax.numpy as jnp
from jax import lax
from jax.experimental import pallas as pl
from jax.experimental.pallas import tpu as pltpu
from jax.sharding import PartitionSpec as P

OBS_BLOCK = 64
F32 = jnp.float32
BF16 = jnp.bfloat16
NT = (((1,), (1,)), ((), ()))


def pieces(x):
    high = x.astype(BF16).astype(F32)
    return high, x - high


def stacked_dot(left, right):
    lh, ll = pieces(left)
    rh, rl = pieces(right)
    lhs = jnp.concatenate([lh, lh, ll], axis=1).astype(BF16)
    rhs = jnp.concatenate([rh, rl, rh], axis=0).astype(BF16)
    return jnp.dot(lhs, rhs, preferred_element_type=F32)


def forecast_kernel(axes, matrix_ref, c_ref, wall_ref, out_ref, x_ref, y_ref, send_sem, land_sem):
    members, fields, cx, cy, nz = c_ref.shape
    nx, ny = axes
    gx, gy = lax.axis_index("gx"), lax.axis_index("gy")
    sides = (
        (gx > 0, (gx - 1, gy), c_ref.at[:, :, 0], x_ref.at[1], x_ref.at[0]),
        (gx < nx - 1, (gx + 1, gy), c_ref.at[:, :, cx - 1], x_ref.at[0], x_ref.at[1]),
        (gy > 0, (gx, gy - 1), c_ref.at[:, :, :, 0, :], y_ref.at[1], y_ref.at[0]),
        (gy < ny - 1, (gx, gy + 1), c_ref.at[:, :, :, cy - 1, :], y_ref.at[0], y_ref.at[1]),
    )
    barrier = pltpu.get_barrier_semaphore()
    for there, peer, _, _, _ in sides:

        @pl.when(there)
        def _():
            pl.semaphore_signal(barrier, inc=1, device_id=peer, device_id_type=pl.DeviceIdType.MESH)

    pl.semaphore_wait(barrier, sum(side[0].astype(jnp.int32) for side in sides))

    def copy(k):
        _, peer, src, dst, _ = sides[k]
        return pltpu.make_async_remote_copy(
            src_ref=src,
            dst_ref=dst,
            send_sem=send_sem.at[k],
            recv_sem=land_sem.at[k ^ 1],
            device_id=peer,
            device_id_type=pl.DeviceIdType.MESH,
        )

    for k, side in enumerate(sides):

        @pl.when(side[0])
        def _():
            copy(k).start()

        @pl.when(jnp.logical_not(side[0]))
        def _():
            side[4][...] = jnp.zeros(side[4].shape, F32)

    for k, side in enumerate(sides):

        @pl.when(side[0])
        def _():
            pltpu.make_async_copy(side[4], side[4], land_sem.at[k]).wait()

    sub = lax.broadcasted_iota(jnp.int32, (cy, nz), 0)
    lane = lax.broadcasted_iota(jnp.int32, (cy, nz), 1)

    def one(m, carry):
        for x in range(cx):
            cells = [c_ref[m, f, x] for f in range(fields)]
            wall = jnp.where(lane == 0, jnp.broadcast_to(wall_ref[m][:, x : x + 1], (cy, nz)), 0.0)
            for f in range(fields):
                c = cells[f]
                before = c_ref[m, f, x - 1] if x > 0 else x_ref[0, m, f]
                after = c_ref[m, f, x + 1] if x < cx - 1 else x_ref[1, m, f]
                lap = before + after
                lap = lap + jnp.where(sub == cy - 1, y_ref[1, m, f, x : x + 1], pltpu.roll(c, cy - 1, 0))
                lap = lap + jnp.where(sub == 0, y_ref[0, m, f, x : x + 1], pltpu.roll(c, 1, 0))
                lap = lap + jnp.where(lane == nz - 1, 0.0, pltpu.roll(c, nz - 1, 1))
                lap = lap + jnp.where(lane == 0, 0.0, pltpu.roll(c, 1, 1)) - 6.0 * c
                slope = 0.5 * (after - before)
                mixed = matrix_ref[f, 0] * cells[0]
                for g in range(1, fields):
                    mixed = mixed + matrix_ref[f, g] * cells[g]
                out_ref[m, f, x] = c + 0.5 * (0.15 * lap - 0.6 * slope + mixed - wall * c)
        return carry

    lax.fori_loop(0, members, one, 0)
    for k, side in enumerate(sides):

        @pl.when(side[0])
        def _():
            copy(k).wait_send()


def forecast(axes, c, wall_texture, matrix):
    members, fields, cx, cy, nz = c.shape
    vmem = pl.BlockSpec(memory_space=pltpu.VMEM)
    return pl.pallas_call(
        functools.partial(forecast_kernel, axes),
        out_shape=jax.ShapeDtypeStruct(c.shape, F32),
        in_specs=[pl.BlockSpec(memory_space=pltpu.SMEM), vmem, vmem],
        out_specs=vmem,
        scratch_shapes=[
            pltpu.VMEM((2, members, fields, cy, nz), F32),
            pltpu.VMEM((2, members, fields, cx, nz), F32),
            pltpu.SemaphoreType.DMA((4,)),
            pltpu.SemaphoreType.DMA((4,)),
        ],
        compiler_params=pltpu.CompilerParams(
            collective_id=1, has_side_effects=True, vmem_limit_bytes=40 * 2**20
        ),
        name="forecast",
    )(matrix, c, wall_texture.transpose(0, 2, 1))


def pick_kernel(nz, field_ref, cell_ref, out_ref, wide_ref):
    members, count = out_ref.shape
    rows = field_ref.shape[0] // members
    cell = cell_ref[0]
    z = lax.rem(cell, nz)
    row = lax.div(cell, nz)
    level = lax.rem(lax.broadcasted_iota(jnp.int32, (2 * nz, count), 0), nz)
    hot = jnp.where(level == z, 1.0, 0.0).astype(BF16)
    wide_ref[...] = jnp.dot(field_ref[...], hot, preferred_element_type=F32)
    total = jnp.zeros((members, count), F32)
    for r in range(rows):
        total = jnp.where(row == r, wide_ref[r * members : (r + 1) * members], total)
    out_ref[...] = total


def pick(first, cells):
    members, rows, nz = first.shape
    batches, obs = cells.shape
    turned = first.transpose(1, 0, 2).reshape(rows * members, nz)
    high = lax.reduce_precision(turned, 8, 7)
    low = (turned - high).astype(BF16)
    high = high.astype(BF16)
    count = min(512, obs)
    return pl.pallas_call(
        functools.partial(pick_kernel, nz),
        grid=(batches, obs // count),
        out_shape=jax.ShapeDtypeStruct((batches, members, obs), F32),
        in_specs=[
            pl.BlockSpec((rows * members, 2 * nz), lambda b, i: (0, 0)),
            pl.BlockSpec((None, 1, count), lambda b, i: (b, 0, i)),
        ],
        out_specs=pl.BlockSpec((None, members, count), lambda b, i: (b, 0, i)),
        scratch_shapes=[pltpu.VMEM((rows * members, count), F32)],
        compiler_params=pltpu.CompilerParams(vmem_limit_bytes=32 * 2**20),
        name="pick",
    )(jnp.concatenate([high, low], axis=1), cells[:, None, :])


def window_kernel(
    axes, y_ref, own_ref, value_ref, var_ref, mask_ref, out_ref, part_ref, send_ref, land_ref,
    masks_ref, send_sem, land_sem, mask_sem
):
    nx, ny = axes
    n = nx * ny
    batches, members, obs = y_ref.shape
    blocks = obs // OBS_BLOCK
    groups = members // 8
    per = min(4, blocks)
    width = per * OBS_BLOCK
    me = lax.axis_index("gx") * ny + lax.axis_index("gy")

    def coords(t):
        return {"gx": lax.div(t, ny), "gy": lax.rem(t, ny)}

    barrier = pltpu.get_barrier_semaphore()

    def greet(d, carry):
        pl.semaphore_signal(
            barrier, inc=1, device_id=coords(lax.rem(me + d, n)), device_id_type=pl.DeviceIdType.MESH
        )
        return carry

    lax.fori_loop(1, n, greet, 0)
    pl.semaphore_wait(barrier, n - 1)

    def share(d, carry):
        pltpu.make_async_remote_copy(
            src_ref=mask_ref,
            dst_ref=masks_ref.at[d - 1],
            send_sem=mask_sem.at[0],
            recv_sem=mask_sem.at[1],
            device_id=coords(lax.rem(me + d, n)),
            device_id_type=pl.DeviceIdType.MESH,
        ).start()
        return carry

    lax.fori_loop(1, n, share, 0)
    masks_ref[n - 1] = mask_ref[...]
    block_of = lax.broadcasted_iota(jnp.int32, (8, width), 1) // OBS_BLOCK
    group_of = lax.broadcasted_iota(jnp.int32, (8, 128), 1) // members
    eye = jnp.where(
        lax.broadcasted_iota(jnp.int32, (members, members), 0)
        == lax.broadcasted_iota(jnp.int32, (members, members), 1),
        1.0,
        0.0,
    )

    def one(b, mix):
        for c in range(obs // width):
            at = pl.ds(c * width, width)
            y = stacked_dot(mix, y_ref[b, :, at])
            ybar = jnp.sum(y, axis=0, keepdims=True) / members
            dev = y - ybar
            spread = jnp.sum(dev * dev, axis=0, keepdims=True) / (members - 1.0)
            var = var_ref[b, :, at]
            total = spread + var
            root = jnp.sqrt(total)
            g = (value_ref[b, :, at] - ybar) / total - dev * (1.0 / (root * (jnp.sqrt(var) + root)))
            g = jnp.where(own_ref[b, :, at] > 0, g, 0.0)
            lhs = jnp.concatenate(
                [
                    jnp.where(block_of == j, g[8 * i : 8 * i + 8], 0.0)
                    for i in range(groups)
                    for j in range(per)
                ],
                axis=0,
            )
            rhs = jnp.concatenate([dev] * groups + [jnp.zeros((128 - groups * members, width), F32)], axis=0)
            lh, ll = pieces(lhs)
            rh, rl = pieces(rhs)
            lh, ll, rh, rl = (a.astype(BF16) for a in (lh, ll, rh, rl))
            dot = functools.partial(lax.dot_general, dimension_numbers=NT, preferred_element_type=F32)
            both = dot(lh, rh) + (dot(lh, rl) + dot(ll, rh))
            for j in range(per):
                tile = jnp.zeros((8, 128), F32)
                for i in range(groups):
                    k = (i * per + j) * 8
                    tile = jnp.where(group_of == i, both[k : k + 8], tile)
                part_ref[c * per + j] = tile

        @pl.when(b == 0)
        def _():
            others = masks_ref.at[pl.ds(0, n - 1)]
            pltpu.make_async_copy(others, others, mask_sem.at[1]).wait()

        mask = masks_ref[:, b, :blocks]
        mask2 = jnp.concatenate([mask, mask], axis=1).astype(BF16)
        for q in range(8):
            high, low = pieces(part_ref[:, q, :])
            send_ref[b, :, q, :] = jnp.dot(
                mask2, jnp.concatenate([high, low], axis=0).astype(BF16), preferred_element_type=F32
            )

        def push(d, carry):
            to = lax.rem(me + d, n)
            pltpu.make_async_remote_copy(
                src_ref=send_ref.at[b, n - 1 - d],
                dst_ref=land_ref.at[b, d - 1],
                send_sem=send_sem.at[b],
                recv_sem=land_sem.at[b],
                device_id=coords(to),
                device_id_type=pl.DeviceIdType.MESH,
            ).start()
            return carry

        lax.fori_loop(1, n, push, 0)
        pltpu.make_async_copy(land_ref.at[b], land_ref.at[b], land_sem.at[b]).wait()
        zsum = send_ref[b, n - 1] + jnp.sum(land_ref[b], axis=0)
        zt = jnp.concatenate(
            [(zsum if i == 0 else pltpu.roll(zsum, 128 - i * members, 1))[:, :members] for i in range(groups)],
            axis=0,
        ) / (members - 1.0)
        zt = zt - jnp.mean(zt, axis=1, keepdims=True)
        pltpu.make_async_copy(land_ref.at[b], land_ref.at[b], send_sem.at[b]).wait()
        return mix + stacked_dot(zt, mix)

    out_ref[...] = lax.fori_loop(0, batches, one, eye)
    others = masks_ref.at[pl.ds(0, n - 1)]
    pltpu.make_async_copy(others, others, mask_sem.at[0]).wait()


def window(axes, y, own, value, var, mask):
    n = axes[0] * axes[1]
    batches, members, obs = y.shape
    vmem = pl.BlockSpec(memory_space=pltpu.VMEM)
    return pl.pallas_call(
        functools.partial(window_kernel, axes),
        out_shape=jax.ShapeDtypeStruct((members, members), F32),
        in_specs=[vmem] * 5,
        out_specs=vmem,
        scratch_shapes=[
            pltpu.VMEM((obs // OBS_BLOCK, 8, 128), F32),
            pltpu.VMEM((batches, n, 8, 128), F32),
            pltpu.VMEM((batches, n - 1, 8, 128), F32),
            pltpu.VMEM((n,) + mask.shape, F32),
            pltpu.SemaphoreType.DMA((batches,)),
            pltpu.SemaphoreType.DMA((batches,)),
            pltpu.SemaphoreType.DMA((2,)),
        ],
        compiler_params=pltpu.CompilerParams(
            collective_id=0, has_side_effects=True, vmem_limit_bytes=40 * 2**20
        ),
        name="window",
    )(y, own[:, None], value[:, None], var[:, None], mask)


def apply_kernel(mix_ref, state_ref, rough_ref, out_ref, rough_out_ref):
    members, fields, cx, cy, nz = state_ref.shape
    mix = mix_ref[...]
    rough_out_ref[...] = stacked_dot(mix, rough_ref[...])
    for x in range(cx):
        for y in range(0, cy, 2):
            cells = jnp.concatenate([state_ref[:, 0, x, y, :], state_ref[:, 0, x, y + 1, :]], axis=1)
            moved = stacked_dot(mix, cells)
            out_ref[:, 0, x, y, :] = moved[:, :nz]
            out_ref[:, 0, x, y + 1, :] = moved[:, nz:]


def apply(mix, state, rough):
    members, fields, cx, cy, nz = state.shape
    block = pl.BlockSpec((members, 1, cx, cy, nz), lambda f: (0, f, 0, 0, 0))
    flat = rough.reshape(members, cx * cy)
    state, flat = pl.pallas_call(
        apply_kernel,
        grid=(fields,),
        out_shape=(
            jax.ShapeDtypeStruct(state.shape, F32),
            jax.ShapeDtypeStruct(flat.shape, F32),
        ),
        in_specs=[
            pl.BlockSpec((members, members), lambda f: (0, 0)),
            block,
            pl.BlockSpec((members, cx * cy), lambda f: (0, 0)),
        ],
        out_specs=(block, pl.BlockSpec((members, cx * cy), lambda f: (0, 0))),
        compiler_params=pltpu.CompilerParams(vmem_limit_bytes=32 * 2**20),
        name="apply",
    )(mix, state, flat)
    return state, flat.reshape(rough.shape)


def on_device(
    axes,
    member_flows,
    wall_texture,
    cross_link_matrix,
    obs_owner,
    obs_cell,
    obs_value,
    obs_var,
    local_mask,
):
    members, fields, cx, cy, nz = member_flows.shape
    mytile = lax.axis_index("gx") * axes[1] + lax.axis_index("gy")
    mask = local_mask[:, 0, 0].astype(F32)
    mask = jnp.pad(mask, ((0, -mask.shape[0] % 8), (0, -mask.shape[1] % 128)))
    own = (obs_owner == mytile).astype(jnp.int32)
    state = forecast(axes, member_flows, wall_texture, cross_link_matrix)
    y = pick(state[:, 0].reshape(members, cx * cy, nz), obs_cell)
    mix = window(axes, y, own, obs_value, obs_var, mask)
    return apply(mix, state, wall_texture)


def solution(mesh):
    axes = (mesh.shape["gx"], mesh.shape["gy"])
    return jax.shard_map(
        functools.partial(on_device, axes),
        mesh=mesh,
        in_specs=(
            P(None, None, "gx", "gy", None),
            P(None, "gx", "gy"),
            P(),
            P(),
            P(),
            P(),
            P(),
            P(None, "gx", "gy", None),
        ),
        out_specs=(P(None, None, "gx", "gy", None), P(None, "gx", "gy")),
        check_vma=False,
    )
```
